32 devices in a mesh: rows: 4 (over x, core), cols: 8 (over z, y).
Axes of the slice: x: 2, y: 2, z: 4, core: 2. Of those that a mesh axis runs over, the one named last changes fastest.
Arguments:
- upper: float32 [4096, 4096], P(('rows', 'cols')), as said below
- matching: int32 [2, 16], replicated, may hold values from 0 to 15, as said below
Outputs:
- rotated: float32 [4096, 4096], P(('rows', 'cols'))
The draws below stay inside these ranges and needn't reach their ends.
Inputs may be any that keep to these rules, and one draw needn't show every extreme that they name: upper is upper triangular: every entry below the diagonal is zero, and every diagonal entry is positive. matching[0] names every block number once; for every row r of matching (round r + 1, r = 0 .. 1), the first block of pair p is that of round 1, matching[r, 2p] = matching[0, 2p], and the second is round 1's second block of pair (p - r) mod (8), matching[r, 2p+1] = matching[0, 2((p - r) mod (8)) + 1].
All inputs are finite; a program needn't handle non-finite values.
Results may differ from the reference program's by a relative error of at most 0.0003.
Values sent between devices are 32-bit elements; how exact they have to be, the bound alone decides.
A program may use at most 128 MiB of HBM per device.

```python
import jax
import jax.numpy as jnp
from jax import lax

BLK = 256
ROUNDS = 2
STEPS = 2
ORDER = 4096
BLOCKS = 16


shared_terms = 16


def draw_matching(key, part):
    first_row = jax.random.permutation(jax.random.fold_in(key, 21), BLOCKS).astype(jnp.int32)
    firsts = first_row[0::2]
    seconds = first_row[1::2]
    rows_out = []
    for round_index in range(ROUNDS):
        moved = jnp.roll(seconds, round_index)
        rows_out.append(jnp.stack([firsts, moved], axis=1).reshape(BLOCKS))
    return jnp.stack(rows_out, axis=0).astype(jnp.int32)


def draw_upper(key, part):
    key_noise = jax.random.fold_in(key, 11)
    key_diag = jax.random.fold_in(key, 12)
    key_left = jax.random.fold_in(key, 13)
    key_right = jax.random.fold_in(key, 14)
    noise_term = jax.random.normal(key_noise, (ORDER, ORDER), jnp.float32)
    diagonal = jax.random.uniform(key_diag, (ORDER,), jnp.float32, 1.0, 2.0)
    share_common = 0.6
    factor_left = jax.random.normal(key_left, (ORDER, shared_terms), jnp.float32)
    factor_right = jax.random.normal(key_right, (shared_terms, ORDER), jnp.float32)
    common = jnp.zeros((ORDER, ORDER), jnp.float32)
    for term_index in range(shared_terms):
        common = common + factor_left[:, term_index:term_index + 1] * factor_right[term_index:term_index + 1, :]
    common = common * (1.0 / shared_terms ** 0.5)
    row_ids = jnp.arange(ORDER)[:, None]
    col_ids = jnp.arange(ORDER)[None, :]
    scale_cols = 1.0 / jnp.sqrt(col_ids.astype(jnp.float32) + 1.0)
    above = ((1.0 - share_common * share_common) ** 0.5 * noise_term + share_common * common) * scale_cols
    matrix = jnp.where(row_ids < col_ids, above, 0.0)
    matrix = matrix + jnp.where(row_ids == col_ids, diagonal[None, :], 0.0)
    return matrix.astype(jnp.float32)


def setup_inputs(seed: int = 0) -> dict:
    splits = jax.random.split(jax.random.key(seed), 3)
    upper = draw_upper(jax.random.fold_in(splits[2], 71), 0)
    matching = draw_matching(jax.random.fold_in(splits[2], 71), 0)
    return dict(upper=upper, matching=matching)


def gram_of(cols_here):
    return lax.dot_general(cols_here.astype(jnp.float32), cols_here.astype(jnp.float32), (((0,), (0,)), ((), ())), precision=lax.Precision.HIGHEST, preferred_element_type=jnp.float32)

def orthonormalize(work_cols):
    lower_factor = jnp.linalg.cholesky(gram_of(work_cols))
    return jax.scipy.linalg.solve_triangular(lower_factor, work_cols.T, lower=True).T

def rotation_of(gram_pair):
    rotation_basis = orthonormalize(gram_pair)
    for step_index in range(STEPS - 1):
        rotation_basis = orthonormalize(jnp.dot(gram_pair.astype(jnp.float32), rotation_basis.astype(jnp.float32), precision=lax.Precision.HIGHEST, preferred_element_type=jnp.float32))
    return rotation_basis

def rotate_columns(pair_cols):
    rotation_basis = rotation_of(gram_of(pair_cols))
    return jnp.dot(pair_cols.astype(jnp.float32), rotation_basis.astype(jnp.float32), precision=lax.Precision.HIGHEST, preferred_element_type=jnp.float32)

def reference(upper, matching):
    matrix = upper
    for round_index in range(ROUNDS):
        order_row = matching[round_index]
        blocks = jnp.take(matrix.reshape(ORDER, BLOCKS, BLK), order_row, axis=1)
        paired = blocks.reshape(ORDER, BLOCKS // 2, 2 * BLK).transpose(1, 0, 2)
        turned = lax.map(rotate_columns, paired)
        unpaired = turned.transpose(1, 0, 2).reshape(ORDER, BLOCKS, BLK)
        inverse_row = jnp.argsort(order_row).astype(jnp.int32)
        matrix = jnp.take(unpaired, inverse_row, axis=1).reshape(ORDER, ORDER)
    return matrix
```

```python
import jax
import jax.numpy as jnp
import numpy as np
from jax import lax
from jax.experimental import pallas as pl
from jax.experimental.pallas import tpu as pltpu
from jax.sharding import PartitionSpec as P

BLK = 256


panel_span = 128


def gram_of(cols_here):
    return lax.dot_general(
        cols_here,
        cols_here,
        (((0,), (0,)), ((), ())),
        precision=lax.Precision.HIGHEST,
        preferred_element_type=jnp.float32,
    )


def product_of(left_mat, right_mat):
    return jnp.dot(
        left_mat, right_mat, precision=lax.Precision.HIGHEST, preferred_element_type=jnp.float32
    )


def blocked_cholesky(gram_mat):
    order_here = gram_mat.shape[0]
    width = min(panel_span, order_here)
    count = order_here // width
    trailing = gram_mat
    columns_out = []
    for panel_index in range(count):
        start = panel_index * width
        diag_part = jnp.linalg.cholesky(trailing[:width, :width])
        below_part = trailing[width:, :width]
        below_factor = jax.scipy.linalg.solve_triangular(diag_part, below_part.T, lower=True).T
        trailing = trailing[width:, width:] - lax.dot_general(
            below_factor,
            below_factor,
            (((1,), (1,)), ((), ())),
            precision=lax.Precision.HIGHEST,
            preferred_element_type=jnp.float32,
        )
        column_panel = jnp.concatenate(
            [jnp.zeros((start, width), jnp.float32), diag_part, below_factor], axis=0
        )
        columns_out.append(column_panel)
    return jnp.concatenate(columns_out, axis=1)


def apply_inverse(work_cols, lower_factor):
    order_here = lower_factor.shape[0]
    width = min(panel_span, order_here)
    count = order_here // width
    solved = []
    for panel_index in range(count):
        start = panel_index * width
        right_side = work_cols[:, start : start + width]
        if panel_index > 0:
            done_cols = jnp.concatenate(solved, axis=1)
            coupling = lower_factor[start : start + width, :start]
            right_side = right_side - lax.dot_general(
                done_cols,
                coupling,
                (((1,), (1,)), ((), ())),
                precision=lax.Precision.HIGHEST,
                preferred_element_type=jnp.float32,
            )
        diag_part = lower_factor[start : start + width, start : start + width]
        solved.append(jax.scipy.linalg.solve_triangular(diag_part, right_side.T, lower=True).T)
    return jnp.concatenate(solved, axis=1)


def orthonormalize(work_cols):
    lower_factor = blocked_cholesky(gram_of(work_cols))
    return apply_inverse(work_cols, lower_factor)


def rotation_of(gram_pair):
    rotation_basis = orthonormalize(gram_pair)
    rotation_basis = orthonormalize(product_of(gram_pair, rotation_basis))
    return rotation_basis


def copy_kernel(order_ref, src_ref, dst_ref):
    dst_ref[...] = src_ref[...].reshape(dst_ref.shape)


def pack_blocks(matrix, order):
    rows, width = matrix.shape
    count = width // BLK
    return pl.pallas_call(
        copy_kernel,
        out_shape=jax.ShapeDtypeStruct((count // 2, rows, 2 * BLK), jnp.float32),
        grid_spec=pltpu.PrefetchScalarGridSpec(
            num_scalar_prefetch=1,
            grid=(count,),
            in_specs=[pl.BlockSpec((rows, BLK), lambda i, order: (0, order[i]))],
            out_specs=pl.BlockSpec((1, rows, BLK), lambda i, order: (i // 2, 0, i % 2)),
        ),
    )(order, matrix)


def unpack_blocks(packed, order):
    pairs, rows, _ = packed.shape
    count = 2 * pairs
    return pl.pallas_call(
        copy_kernel,
        out_shape=jax.ShapeDtypeStruct((rows, count * BLK), jnp.float32),
        grid_spec=pltpu.PrefetchScalarGridSpec(
            num_scalar_prefetch=1,
            grid=(count,),
            in_specs=[pl.BlockSpec((1, rows, BLK), lambda i, order: (i // 2, 0, i % 2))],
            out_specs=pl.BlockSpec((rows, BLK), lambda i, order: (0, order[i])),
        ),
    )(order, packed)


def pair_places(count):
    half = count // 2
    return [2 * k if k < half else 2 * (count - 1 - k) + 1 for k in range(count)]


def pair_round(owned_pair):
    gram_terms = gram_of(owned_pair)
    rotation_basis = rotation_of(lax.psum(gram_terms, "rows"))
    return product_of(owned_pair, rotation_basis)


def exchange(chunks):
    return lax.all_to_all(chunks, "cols", split_axis=0, concat_axis=0, tiled=True)


def make_body(count):
    places = pair_places(count)
    pair_at = np.argsort(np.array(places))
    slots = np.stack([2 * pair_at, 2 * pair_at + 1], axis=1).reshape(-1)
    ring = [(places[k], places[(k + 1) % count]) for k in range(count)]

    def body(upper, matching):
        rows = upper.shape[0]
        chunks = exchange(pack_blocks(upper, matching[0][slots]))
        owned = chunks.reshape(count * rows, 2 * BLK)
        owned = pair_round(owned)
        second = lax.ppermute(owned[:, BLK:], "cols", ring)
        owned = jnp.concatenate([owned[:, :BLK], second], axis=1)
        owned = pair_round(owned)
        returned = exchange(owned.reshape(count, rows, 2 * BLK))
        return unpack_blocks(returned, matching[1][slots])

    return body


def solution(mesh):
    in_specs = (P(("rows", "cols"), None), P())
    out_specs = P(("rows", "cols"), None)
    return jax.shard_map(
        make_body(mesh.shape["cols"]),
        mesh=mesh,
        in_specs=in_specs,
        out_specs=out_specs,
        check_vma=False,
    )
```

```python
import functools

import jax
import jax.numpy as jnp
import numpy as np
from jax import lax
from jax.experimental import pallas as pl
from jax.experimental.pallas import tpu as pltpu
from jax.sharding import PartitionSpec as P

BLK = 256
HIGH = lax.Precision.HIGHEST
SUB, WIDE = 8, 128


def wide(part):
    return jnp.broadcast_to(part, (SUB, WIDE))


def factor_panel(diag):
    count = WIDE // SUB
    row = lax.broadcasted_iota(jnp.int32, (SUB, WIDE), 0)
    lane = lax.broadcasted_iota(jnp.int32, (SUB, WIDE), 1)
    left = [diag[SUB * k : SUB * (k + 1), :] for k in range(count)]
    right = [jnp.where(lane == row + SUB * k, 1.0, 0.0) for k in range(count)]

    def columns_of(tile, b):
        return [wide(tile[:, SUB * b + i : SUB * b + i + 1]) for i in range(SUB)]

    for b in range(count):
        here, mirror = left[b], right[b]
        cols = columns_of(here, b)
        scale = jnp.zeros((SUB, WIDE), jnp.float32)
        left_rows, right_rows, pivots, cross = [], [], [], []
        for i in range(SUB):
            root = lax.rsqrt(wide(cols[i][i : i + 1, :]))
            inverse = root * root
            scale = jnp.where(row == i, root, scale)
            left_rows.append(wide(here[i : i + 1, :]))
            right_rows.append(wide(mirror[i : i + 1, :]))
            pivots.append(inverse)
            cross.append([wide(cols[j][i : i + 1, :]) for j in range(i + 1, SUB)])
            if i + 1 < SUB:
                factor = jnp.where(row > i, cols[i] * inverse, 0.0)
                for j in range(i + 1, SUB):
                    cols[j] = cols[j] - factor * cross[i][j - i - 1]
                here = here - factor * left_rows[i]
                mirror = mirror - factor * right_rows[i]
        right[b] = mirror * scale
        for k in range(b + 1, count):
            below = columns_of(left[k], b)
            for i in range(SUB):
                factor = below[i] * pivots[i]
                for j in range(i + 1, SUB):
                    below[j] = below[j] - factor * cross[i][j - i - 1]
                left[k] = left[k] - factor * left_rows[i]
                right[k] = right[k] - factor * right_rows[i]
    return jnp.concatenate(right, axis=0)


def mul(a, b, dims):
    return lax.dot_general(
        a, b, (dims, ((), ())), precision=HIGH, preferred_element_type=jnp.float32
    )


def rotation_kernel(steps, gram_ref, turn_ref, work_ref, inv_ref):
    n = gram_ref.shape[0]
    count = n // WIDE

    def panel(t, carry):
        p = lax.rem(t, count)

        @pl.when(t == 0)
        def _():
            work_ref[:, n:] = gram_ref[...]

        @pl.when(jnp.logical_and(p == 0, t > 0))
        def _():
            work_ref[:, n:] = mul(work_ref[:, n:], gram_ref[...], ((1,), (0,)))

        @pl.when(p == 0)
        def _():
            work_ref[:, :n] = mul(work_ref[:, n:], work_ref[:, n:], ((1,), (1,)))

        at = pl.ds(pl.multiple_of(p * WIDE, WIDE), WIDE)
        inv_ref[...] = factor_panel(work_ref[at, at])
        for q in range(count):

            @pl.when(p == q)
            def _():
                lo, hi = q * WIDE, (q + 1) * WIDE
                rows = mul(inv_ref[...], work_ref[lo:hi, hi:], ((1,), (0,)))
                work_ref[lo:hi, hi:] = rows
                if q + 1 < count:
                    work_ref[hi:, hi:] -= mul(rows[:, : n - hi], rows, ((0,), (0,)))

        return carry

    lax.fori_loop(0, steps * count, panel, 0)
    turn_ref[...] = work_ref[:, n:]


def rotation_of(gram):
    n = gram.shape[0]
    return pl.pallas_call(
        functools.partial(rotation_kernel, 2),
        out_shape=jax.ShapeDtypeStruct((n, n), jnp.float32),
        in_specs=[pl.BlockSpec(memory_space=pltpu.VMEM)],
        out_specs=pl.BlockSpec(memory_space=pltpu.VMEM),
        scratch_shapes=[
            pltpu.VMEM((n, 2 * n), jnp.float32),
            pltpu.VMEM((WIDE, WIDE), jnp.float32),
        ],
        compiler_params=pltpu.CompilerParams(vmem_limit_bytes=48 * 2**20),
    )(gram)


def gram_of(cols_here):
    return lax.dot_general(
        cols_here,
        cols_here,
        (((0,), (0,)), ((), ())),
        precision=HIGH,
        preferred_element_type=jnp.float32,
    )


def pack_kernel(order_ref, src_ref, dst_ref, sem):
    copies = [
        pltpu.make_async_copy(
            src_ref.at[:, pl.ds(pl.multiple_of(order_ref[i] * BLK, BLK), BLK)],
            dst_ref.at[i // 2, :, pl.ds(i % 2 * BLK, BLK)],
            sem.at[i],
        )
        for i in range(order_ref.shape[0])
    ]
    for copy in copies:
        copy.start()
    for copy in copies:
        copy.wait()


def unpack_kernel(order_ref, src_ref, dst_ref, sem):
    copies = [
        pltpu.make_async_copy(
            src_ref.at[i // 2, :, pl.ds(i % 2 * BLK, BLK)],
            dst_ref.at[:, pl.ds(pl.multiple_of(order_ref[i] * BLK, BLK), BLK)],
            sem.at[i],
        )
        for i in range(order_ref.shape[0])
    ]
    for copy in copies:
        copy.start()
    for copy in copies:
        copy.wait()


def move_blocks(kernel, array, order, shape):
    return pl.pallas_call(
        kernel,
        out_shape=jax.ShapeDtypeStruct(shape, jnp.float32),
        in_specs=[
            pl.BlockSpec(memory_space=pltpu.SMEM),
            pl.BlockSpec(memory_space=pl.ANY),
        ],
        out_specs=pl.BlockSpec(memory_space=pl.ANY),
        scratch_shapes=[pltpu.SemaphoreType.DMA((order.shape[0],))],
    )(order, array)


def pack_blocks(matrix, order):
    rows, width = matrix.shape
    return move_blocks(pack_kernel, matrix, order, (width // (2 * BLK), rows, 2 * BLK))


def unpack_blocks(packed, order):
    pairs, rows, span = packed.shape
    return move_blocks(unpack_kernel, packed, order, (rows, pairs * span))


def pair_places(count):
    half = count // 2
    return [2 * k if k < half else 2 * (count - 1 - k) + 1 for k in range(count)]


def pair_round(owned_pair):
    turn = rotation_of(lax.psum(gram_of(owned_pair), "rows"))
    return mul(owned_pair, turn, ((1,), (1,)))


def exchange(chunks):
    return lax.all_to_all(chunks, "cols", split_axis=0, concat_axis=0, tiled=True)


def make_body(count):
    places = pair_places(count)
    pair_at = np.argsort(np.array(places))
    slots = np.stack([2 * pair_at, 2 * pair_at + 1], axis=1).reshape(-1)
    ring = [(places[k], places[(k + 1) % count]) for k in range(count)]

    def body(upper, matching):
        rows = upper.shape[0]
        chunks = exchange(pack_blocks(upper, matching[0][slots]))
        owned = chunks.reshape(count * rows, 2 * BLK)
        owned = pair_round(owned)
        second = lax.ppermute(owned[:, BLK:], "cols", ring)
        owned = jnp.concatenate([owned[:, :BLK], second], axis=1)
        owned = pair_round(owned)
        returned = exchange(owned.reshape(count, rows, 2 * BLK))
        return unpack_blocks(returned, matching[1][slots])

    return body


def solution(mesh):
    in_specs = (P(("rows", "cols"), None), P())
    out_specs = P(("rows", "cols"), None)
    return jax.shard_map(
        make_body(mesh.shape["cols"]),
        mesh=mesh,
        in_specs=in_specs,
        out_specs=out_specs,
        check_vma=False,
    )
```

```python
import functools

import jax
import jax.numpy as jnp
import numpy as np
from jax import lax
from jax.experimental import pallas as pl
from jax.experimental.pallas import tpu as pltpu
from jax.sharding import PartitionSpec as P

BLK = 256
HIGH = lax.Precision.HIGHEST
SUB, WIDE = 8, 128


def wide(part):
    return jnp.broadcast_to(part, (SUB, WIDE))


def factor_panel(diag):
    count = WIDE // SUB
    row = lax.broadcasted_iota(jnp.int32, (SUB, WIDE), 0)
    lane = lax.broadcasted_iota(jnp.int32, (SUB, WIDE), 1)
    left = [diag[SUB * k : SUB * (k + 1), :] for k in range(count)]
    right = [jnp.where(lane == row + SUB * k, 1.0, 0.0) for k in range(count)]

    def columns_of(tile, b):
        return [wide(tile[:, SUB * b + i : SUB * b + i + 1]) for i in range(SUB)]

    for b in range(count):
        here, mirror = left[b], right[b]
        cols = columns_of(here, b)
        scale = jnp.zeros((SUB, WIDE), jnp.float32)
        left_rows, right_rows, pivots, cross = [], [], [], []
        for i in range(SUB):
            root = lax.rsqrt(wide(cols[i][i : i + 1, :]))
            inverse = root * root
            scale = jnp.where(row == i, root, scale)
            left_rows.append(wide(here[i : i + 1, :]))
            right_rows.append(wide(mirror[i : i + 1, :]))
            pivots.append(inverse)
            cross.append([wide(cols[j][i : i + 1, :]) for j in range(i + 1, SUB)])
            if i + 1 < SUB:
                factor = jnp.where(row > i, cols[i] * inverse, 0.0)
                for j in range(i + 1, SUB):
                    cols[j] = cols[j] - factor * cross[i][j - i - 1]
                here = here - factor * left_rows[i]
                mirror = mirror - factor * right_rows[i]
        right[b] = mirror * scale
        for k in range(b + 1, count):
            below = columns_of(left[k], b)
            for i in range(SUB):
                factor = below[i] * pivots[i]
                for j in range(i + 1, SUB):
                    below[j] = below[j] - factor * cross[i][j - i - 1]
                left[k] = left[k] - factor * left_rows[i]
                right[k] = right[k] - factor * right_rows[i]
    return jnp.concatenate(right, axis=0)


def mul(a, b, dims):
    return lax.dot_general(
        a, b, (dims, ((), ())), precision=HIGH, preferred_element_type=jnp.float32
    )


def rotation_kernel(steps, gram_ref, turn_ref, work_ref, inv_ref):
    n = gram_ref.shape[0]
    count = n // WIDE

    def panel(t, carry):
        p = lax.rem(t, count)

        @pl.when(t == 0)
        def _():
            work_ref[:, n:] = gram_ref[...]

        @pl.when(jnp.logical_and(p == 0, t > 0))
        def _():
            work_ref[:, n:] = mul(work_ref[:, n:], gram_ref[...], ((1,), (0,)))

        @pl.when(p == 0)
        def _():
            work_ref[:, :n] = mul(work_ref[:, n:], work_ref[:, n:], ((1,), (1,)))

        at = pl.ds(pl.multiple_of(p * WIDE, WIDE), WIDE)
        inv_ref[...] = factor_panel(work_ref[at, at])
        for q in range(count):

            @pl.when(p == q)
            def _():
                lo, hi = q * WIDE, (q + 1) * WIDE
                rows = mul(inv_ref[...], work_ref[lo:hi, hi:], ((1,), (0,)))
                work_ref[lo:hi, hi:] = rows
                if q + 1 < count:
                    work_ref[hi:, hi:] -= mul(rows[:, : n - hi], rows, ((0,), (0,)))

        return carry

    lax.fori_loop(0, steps * count, panel, 0)
    turn_ref[...] = work_ref[:, n:]


def rotation_of(gram):
    n = gram.shape[0]
    return pl.pallas_call(
        functools.partial(rotation_kernel, 2),
        out_shape=jax.ShapeDtypeStruct((n, n), jnp.float32),
        in_specs=[pl.BlockSpec(memory_space=pltpu.VMEM)],
        out_specs=pl.BlockSpec(memory_space=pltpu.VMEM),
        scratch_shapes=[
            pltpu.VMEM((n, 2 * n), jnp.float32),
            pltpu.VMEM((WIDE, WIDE), jnp.float32),
        ],
        compiler_params=pltpu.CompilerParams(vmem_limit_bytes=48 * 2**20),
    )(gram)


def gram_of(cols_here):
    return lax.dot_general(
        cols_here,
        cols_here,
        (((0,), (0,)), ((), ())),
        precision=HIGH,
        preferred_element_type=jnp.float32,
    )


def pack_kernel(order_ref, src_ref, dst_ref):
    for i in range(order_ref.shape[0]):
        at = pl.ds(pl.multiple_of(order_ref[i] * BLK, BLK), BLK)
        dst_ref[i // 2, :, pl.ds(i % 2 * BLK, BLK)] = src_ref[:, at]


def unpack_kernel(order_ref, src_ref, dst_ref):
    for i in range(order_ref.shape[0]):
        at = pl.ds(pl.multiple_of(order_ref[i] * BLK, BLK), BLK)
        dst_ref[:, at] = src_ref[i // 2, :, pl.ds(i % 2 * BLK, BLK)]


def move_blocks(kernel, array, order, shape):
    return pl.pallas_call(
        kernel,
        out_shape=jax.ShapeDtypeStruct(shape, jnp.float32),
        in_specs=[
            pl.BlockSpec(memory_space=pltpu.SMEM),
            pl.BlockSpec(memory_space=pltpu.VMEM),
        ],
        out_specs=pl.BlockSpec(memory_space=pltpu.VMEM),
        compiler_params=pltpu.CompilerParams(vmem_limit_bytes=48 * 2**20),
    )(order, array)


def pack_blocks(matrix, order):
    rows, width = matrix.shape
    return move_blocks(pack_kernel, matrix, order, (width // (2 * BLK), rows, 2 * BLK))


def unpack_blocks(packed, order):
    pairs, rows, span = packed.shape
    return move_blocks(unpack_kernel, packed, order, (rows, pairs * span))


def pair_places(rows, low):
    path = [0, 1, 3, 2] if rows == 4 else list(range(rows))
    places = []
    for at in range(low):
        places += [r * low + at for r in (path if at % 2 == 0 else path[::-1])]
    return places


GROUP = ("rows", "low")


def pair_round(owned_pair):
    turn = rotation_of(lax.psum(gram_of(owned_pair), "high"))
    return mul(owned_pair, turn, ((1,), (1,)))


def exchange(chunks):
    return lax.all_to_all(chunks, GROUP, split_axis=0, concat_axis=0, tiled=True)


def make_body(rows, low):
    count = rows * low
    places = pair_places(rows, low)
    pair_at = np.argsort(np.array(places))
    slots = np.stack([2 * pair_at, 2 * pair_at + 1], axis=1).reshape(-1)
    ring = [(places[k], places[(k + 1) % count]) for k in range(count)]

    def body(upper, matching):
        deep = upper.shape[0]
        chunks = exchange(pack_blocks(upper, matching[0][slots]))
        owned = pair_round(chunks.reshape(count * deep, 2 * BLK))
        second = lax.ppermute(owned[:, BLK:], GROUP, ring)
        owned = pair_round(jnp.concatenate([owned[:, :BLK], second], axis=1))
        returned = exchange(owned.reshape(count, deep, 2 * BLK))
        return unpack_blocks(returned, matching[1][slots])

    return body


def solution(mesh):
    rows, cols = mesh.shape["rows"], mesh.shape["cols"]
    low = cols // rows
    split = jax.sharding.Mesh(mesh.devices.reshape(rows, cols // low, low), ("rows", "high", "low"))
    spec = P(("rows", "high", "low"), None)
    return jax.shard_map(
        make_body(rows, low), mesh=split, in_specs=(spec, P()), out_specs=spec, check_vma=False
    )
```

```python
import functools

import jax
import jax.numpy as jnp
import numpy as np
from jax import lax
from jax.experimental import pallas as pl
from jax.experimental.pallas import tpu as pltpu
from jax.sharding import PartitionSpec as P

BLK = 256
HIGH = lax.Precision.HIGHEST
SUB, WIDE = 8, 128


def wide(part):
    return jnp.broadcast_to(part, (SUB, WIDE))


def factor_panel(diag):
    count = WIDE // SUB
    row = lax.broadcasted_iota(jnp.int32, (SUB, WIDE), 0)
    lane = lax.broadcasted_iota(jnp.int32, (SUB, WIDE), 1)
    left = [diag[SUB * k : SUB * (k + 1), :] for k in range(count)]
    right = [jnp.where(lane == row + SUB * k, 1.0, 0.0) for k in range(count)]

    def columns_of(tile, b):
        return [wide(tile[:, SUB * b + i : SUB * b + i + 1]) for i in range(SUB)]

    for b in range(count):
        here, mirror = left[b], right[b]
        cols = columns_of(here, b)
        scale = jnp.zeros((SUB, WIDE), jnp.float32)
        left_rows, right_rows, pivots, cross = [], [], [], []
        for i in range(SUB):
            root = lax.rsqrt(wide(cols[i][i : i + 1, :]))
            inverse = root * root
            scale = jnp.where(row == i, root, scale)
            left_rows.append(wide(here[i : i + 1, :]))
            right_rows.append(wide(mirror[i : i + 1, :]))
            pivots.append(inverse)
            cross.append([wide(cols[j][i : i + 1, :]) for j in range(i + 1, SUB)])
            if i + 1 < SUB:
                factor = jnp.where(row > i, cols[i] * inverse, 0.0)
                for j in range(i + 1, SUB):
                    cols[j] = cols[j] - factor * cross[i][j - i - 1]
                here = here - factor * left_rows[i]
                mirror = mirror - factor * right_rows[i]
        right[b] = mirror * scale
        for k in range(b + 1, count):
            below = columns_of(left[k], b)
            for i in range(SUB):
                factor = below[i] * pivots[i]
                for j in range(i + 1, SUB):
                    below[j] = below[j] - factor * cross[i][j - i - 1]
                left[k] = left[k] - factor * left_rows[i]
                right[k] = right[k] - factor * right_rows[i]
    return jnp.concatenate(right, axis=0)


def mul(a, b, dims):
    return lax.dot_general(
        a, b, (dims, ((), ())), precision=HIGH, preferred_element_type=jnp.float32
    )


def rotation_kernel(steps, gram_ref, turn_ref, work_ref, inv_ref):
    n = gram_ref.shape[0]
    count = n // WIDE

    def panel(t, carry):
        p = lax.rem(t, count)

        @pl.when(t == 0)
        def _():
            work_ref[:, n:] = gram_ref[...]

        @pl.when(jnp.logical_and(p == 0, t > 0))
        def _():
            work_ref[:, n:] = mul(work_ref[:, n:], gram_ref[...], ((1,), (0,)))

        @pl.when(p == 0)
        def _():
            work_ref[:, :n] = mul(work_ref[:, n:], work_ref[:, n:], ((1,), (1,)))

        at = pl.ds(pl.multiple_of(p * WIDE, WIDE), WIDE)
        inv_ref[...] = factor_panel(work_ref[at, at])
        for q in range(count):

            @pl.when(p == q)
            def _():
                lo, hi = q * WIDE, (q + 1) * WIDE
                rows = mul(inv_ref[...], work_ref[lo:hi, hi:], ((1,), (0,)))
                work_ref[lo:hi, hi:] = rows
                if q + 1 < count:
                    work_ref[hi:, hi:] -= mul(rows[:, : n - hi], rows, ((0,), (0,)))

        return carry

    lax.fori_loop(0, steps * count, panel, 0)
    turn_ref[...] = work_ref[:, n:]


def rotation_of(gram):
    n = gram.shape[0]
    return pl.pallas_call(
        functools.partial(rotation_kernel, 2),
        out_shape=jax.ShapeDtypeStruct((n, n), jnp.float32),
        in_specs=[pl.BlockSpec(memory_space=pltpu.VMEM)],
        out_specs=pl.BlockSpec(memory_space=pltpu.VMEM),
        scratch_shapes=[
            pltpu.VMEM((n, 2 * n), jnp.float32),
            pltpu.VMEM((WIDE, WIDE), jnp.float32),
        ],
        compiler_params=pltpu.CompilerParams(vmem_limit_bytes=48 * 2**20),
    )(gram)


def gram_of(cols_here):
    return lax.dot_general(
        cols_here,
        cols_here,
        (((0,), (0,)), ((), ())),
        precision=HIGH,
        preferred_element_type=jnp.float32,
    )


def sum_kernel(peers, gram_ref, out_ref, mine, total, landed, sems):
    tiles = gram_ref.shape[0] // WIDE
    upper = [(i, j) for i in range(tiles) for j in range(i, tiles)]
    share = len(upper) * WIDE // peers
    me = lax.axis_index("high")
    for t, (i, j) in enumerate(upper):
        mine[t * WIDE : (t + 1) * WIDE, :] = gram_ref[
            i * WIDE : (i + 1) * WIDE, j * WIDE : (j + 1) * WIDE
        ]
    others = [lax.rem(me + k, peers) for k in range(1, peers)]
    barrier = pltpu.get_barrier_semaphore()
    for other in others:
        pl.semaphore_signal(
            barrier, inc=1, device_id={"high": other}, device_id_type=pl.DeviceIdType.MESH
        )
    pl.semaphore_wait(barrier, peers - 1)

    def part(who):
        return pl.ds(pl.multiple_of(who * share, SUB), share)

    def send(src, dst, phase, k):
        return pltpu.make_async_remote_copy(
            src_ref=src,
            dst_ref=dst,
            send_sem=sems.at[2 * phase, k],
            recv_sem=sems.at[2 * phase + 1, k],
            device_id={"high": others[k]},
            device_id_type=pl.DeviceIdType.MESH,
        )

    scatter = [send(mine.at[part(others[k])], landed.at[k], 0, k) for k in range(peers - 1)]
    for copy in scatter:
        copy.start()
    whole = mine[part(me), :]
    for k, copy in enumerate(scatter):
        copy.wait_recv()
        whole = whole + landed[k]
    total[part(me), :] = whole
    gather = [send(total.at[part(me)], total.at[part(me)], 1, k) for k in range(peers - 1)]
    for copy in gather:
        copy.start()
    for copy in scatter:
        copy.wait_send()
    for copy in gather:
        copy.wait()
    for t, (i, j) in enumerate(upper):
        tile = total[t * WIDE : (t + 1) * WIDE, :]
        out_ref[i * WIDE : (i + 1) * WIDE, j * WIDE : (j + 1) * WIDE] = tile
        if j > i:
            out_ref[j * WIDE : (j + 1) * WIDE, i * WIDE : (i + 1) * WIDE] = tile.T


def summed(gram, peers):
    n = gram.shape[0]
    tiles = n // WIDE
    deep = tiles * (tiles + 1) // 2 * WIDE
    return pl.pallas_call(
        functools.partial(sum_kernel, peers),
        out_shape=jax.ShapeDtypeStruct((n, n), jnp.float32),
        in_specs=[pl.BlockSpec(memory_space=pltpu.VMEM)],
        out_specs=pl.BlockSpec(memory_space=pltpu.VMEM),
        scratch_shapes=[
            pltpu.VMEM((deep, WIDE), jnp.float32),
            pltpu.VMEM((deep, WIDE), jnp.float32),
            pltpu.VMEM((peers - 1, deep // peers, WIDE), jnp.float32),
            pltpu.SemaphoreType.DMA((4, peers - 1)),
        ],
        compiler_params=pltpu.CompilerParams(
            collective_id=0, has_side_effects=True, vmem_limit_bytes=32 * 2**20
        ),
    )(gram)


def pack_kernel(order_ref, src_ref, dst_ref):
    for i in range(order_ref.shape[0]):
        at = pl.ds(pl.multiple_of(order_ref[i] * BLK, BLK), BLK)
        dst_ref[i // 2, :, pl.ds(i % 2 * BLK, BLK)] = src_ref[:, at]


def unpack_kernel(order_ref, src_ref, dst_ref):
    for i in range(order_ref.shape[0]):
        at = pl.ds(pl.multiple_of(order_ref[i] * BLK, BLK), BLK)
        dst_ref[:, at] = src_ref[i // 2, :, pl.ds(i % 2 * BLK, BLK)]


def move_blocks(kernel, array, order, shape):
    return pl.pallas_call(
        kernel,
        out_shape=jax.ShapeDtypeStruct(shape, jnp.float32),
        in_specs=[
            pl.BlockSpec(memory_space=pltpu.SMEM),
            pl.BlockSpec(memory_space=pltpu.VMEM),
        ],
        out_specs=pl.BlockSpec(memory_space=pltpu.VMEM),
        compiler_params=pltpu.CompilerParams(vmem_limit_bytes=48 * 2**20),
    )(order, array)


def pack_blocks(matrix, order):
    rows, width = matrix.shape
    return move_blocks(pack_kernel, matrix, order, (width // (2 * BLK), rows, 2 * BLK))


def unpack_blocks(packed, order):
    pairs, rows, span = packed.shape
    return move_blocks(unpack_kernel, packed, order, (rows, pairs * span))


def pair_places(rows, low):
    path = [0, 1, 3, 2] if rows == 4 else list(range(rows))
    places = []
    for at in range(low):
        places += [r * low + at for r in (path if at % 2 == 0 else path[::-1])]
    return places


GROUP = ("rows", "low")


def pair_round(owned_pair, high):
    turn = rotation_of(summed(gram_of(owned_pair), high))
    return mul(owned_pair, turn, ((1,), (1,)))


def exchange(chunks):
    return lax.all_to_all(chunks, GROUP, split_axis=0, concat_axis=0, tiled=True)


def make_body(rows, high, low):
    count = rows * low
    places = pair_places(rows, low)
    pair_at = np.argsort(np.array(places))
    slots = np.stack([2 * pair_at, 2 * pair_at + 1], axis=1).reshape(-1)
    ring = [(places[k], places[(k + 1) % count]) for k in range(count)]

    def body(upper, matching):
        deep = upper.shape[0]
        chunks = exchange(pack_blocks(upper, matching[0][slots]))
        owned = pair_round(chunks.reshape(count * deep, 2 * BLK), high)
        second = lax.ppermute(owned[:, BLK:], GROUP, ring)
        owned = pair_round(jnp.concatenate([owned[:, :BLK], second], axis=1), high)
        returned = exchange(owned.reshape(count, deep, 2 * BLK))
        return unpack_blocks(returned, matching[1][slots])

    return body


def solution(mesh):
    rows, cols = mesh.shape["rows"], mesh.shape["cols"]
    low = cols // rows
    high = cols // low
    split = jax.sharding.Mesh(mesh.devices.reshape(rows, high, low), ("rows", "high", "low"))
    spec = P(("rows", "high", "low"), None)
    return jax.shard_map(
        make_body(rows, high, low), mesh=split, in_specs=(spec, P()), out_specs=spec, check_vma=False
    )
```

```python
import functools

import jax
import jax.numpy as jnp
import numpy as np
from jax import lax
from jax.experimental import pallas as pl
from jax.experimental.pallas import tpu as pltpu
from jax.sharding import PartitionSpec as P

BLK = 256
HIGH = lax.Precision.HIGHEST
SUB, WIDE = 8, 128


def wide(part):
    return jnp.broadcast_to(part, (SUB, WIDE))


def factor_panel(diag):
    count = WIDE // SUB
    row = lax.broadcasted_iota(jnp.int32, (SUB, WIDE), 0)
    lane = lax.broadcasted_iota(jnp.int32, (SUB, WIDE), 1)
    left = [diag[SUB * k : SUB * (k + 1), :] for k in range(count)]
    right = [jnp.where(lane == row + SUB * k, 1.0, 0.0) for k in range(count)]

    def columns_of(tile, b):
        return [wide(tile[:, SUB * b + i : SUB * b + i + 1]) for i in range(SUB)]

    for b in range(count):
        here, mirror = left[b], right[b]
        cols = columns_of(here, b)
        scale = jnp.zeros((SUB, WIDE), jnp.float32)
        left_rows, right_rows, pivots, cross = [], [], [], []
        for i in range(SUB):
            root = lax.rsqrt(wide(cols[i][i : i + 1, :]))
            inverse = root * root
            scale = jnp.where(row == i, root, scale)
            left_rows.append(wide(here[i : i + 1, :]))
            right_rows.append(wide(mirror[i : i + 1, :]))
            pivots.append(inverse)
            cross.append([wide(cols[j][i : i + 1, :]) for j in range(i + 1, SUB)])
            if i + 1 < SUB:
                factor = jnp.where(row > i, cols[i] * inverse, 0.0)
                for j in range(i + 1, SUB):
                    cols[j] = cols[j] - factor * cross[i][j - i - 1]
                here = here - factor * left_rows[i]
                mirror = mirror - factor * right_rows[i]
        right[b] = mirror * scale
        for k in range(b + 1, count):
            below = columns_of(left[k], b)
            for i in range(SUB):
                factor = below[i] * pivots[i]
                for j in range(i + 1, SUB):
                    below[j] = below[j] - factor * cross[i][j - i - 1]
                left[k] = left[k] - factor * left_rows[i]
                right[k] = right[k] - factor * right_rows[i]
    return jnp.concatenate(right, axis=0)


def mul(a, b, dims):
    return lax.dot_general(
        a, b, (dims, ((), ())), precision=HIGH, preferred_element_type=jnp.float32
    )


def rotation_kernel(steps, gram_ref, turn_ref, work_ref, inv_ref):
    n = gram_ref.shape[0]
    count = n // WIDE

    def panel(t, carry):
        p = lax.rem(t, count)

        @pl.when(t == 0)
        def _():
            work_ref[:, n:] = gram_ref[...]

        @pl.when(jnp.logical_and(p == 0, t > 0))
        def _():
            work_ref[:, n:] = mul(work_ref[:, n:], gram_ref[...], ((1,), (0,)))

        @pl.when(p == 0)
        def _():
            work_ref[:, :n] = mul(work_ref[:, n:], work_ref[:, n:], ((1,), (1,)))

        at = pl.ds(pl.multiple_of(p * WIDE, WIDE), WIDE)
        inv_ref[...] = factor_panel(work_ref[at, at])
        for q in range(count):

            @pl.when(p == q)
            def _():
                lo, hi = q * WIDE, (q + 1) * WIDE
                rows = mul(inv_ref[...], work_ref[lo:hi, hi:], ((1,), (0,)))
                work_ref[lo:hi, hi:] = rows
                if q + 1 < count:
                    work_ref[hi:, hi:] -= mul(rows[:, : n - hi], rows, ((0,), (0,)))

        return carry

    lax.fori_loop(0, steps * count, panel, 0)
    turn_ref[...] = work_ref[:, n:]


def rotation_of(gram):
    n = gram.shape[0]
    return pl.pallas_call(
        functools.partial(rotation_kernel, 2),
        out_shape=jax.ShapeDtypeStruct((n, n), jnp.float32),
        in_specs=[pl.BlockSpec(memory_space=pltpu.VMEM)],
        out_specs=pl.BlockSpec(memory_space=pltpu.VMEM),
        scratch_shapes=[
            pltpu.VMEM((n, 2 * n), jnp.float32),
            pltpu.VMEM((WIDE, WIDE), jnp.float32),
        ],
        compiler_params=pltpu.CompilerParams(vmem_limit_bytes=48 * 2**20),
    )(gram)


def gram_of(cols_here):
    return lax.dot_general(
        cols_here,
        cols_here,
        (((0,), (0,)), ((), ())),
        precision=HIGH,
        preferred_element_type=jnp.float32,
    )


def sum_kernel(peers, gram_ref, out_ref, mine, total, landed, sems):
    tiles = gram_ref.shape[0] // WIDE
    upper = [(i, j) for i in range(tiles) for j in range(i, tiles)]
    share = len(upper) * WIDE // peers
    me = lax.axis_index("high")
    for t, (i, j) in enumerate(upper):
        mine[t * WIDE : (t + 1) * WIDE, :] = gram_ref[
            i * WIDE : (i + 1) * WIDE, j * WIDE : (j + 1) * WIDE
        ]
    others = [lax.rem(me + k, peers) for k in range(1, peers)]
    barrier = pltpu.get_barrier_semaphore()
    for other in others:
        pl.semaphore_signal(
            barrier, inc=1, device_id={"high": other}, device_id_type=pl.DeviceIdType.MESH
        )
    pl.semaphore_wait(barrier, peers - 1)

    def part(who):
        return pl.ds(pl.multiple_of(who * share, SUB), share)

    def send(src, dst, phase, k):
        return pltpu.make_async_remote_copy(
            src_ref=src,
            dst_ref=dst,
            send_sem=sems.at[2 * phase, k],
            recv_sem=sems.at[2 * phase + 1, k],
            device_id={"high": others[k]},
            device_id_type=pl.DeviceIdType.MESH,
        )

    scatter = [send(mine.at[part(others[k])], landed.at[k], 0, k) for k in range(peers - 1)]
    for copy in scatter:
        copy.start()
    whole = mine[part(me), :]
    for k, copy in enumerate(scatter):
        copy.wait_recv()
        whole = whole + landed[k]
    total[part(me), :] = whole
    gather = [send(total.at[part(me)], total.at[part(me)], 1, k) for k in range(peers - 1)]
    for copy in gather:
        copy.start()
    for copy in scatter:
        copy.wait_send()
    for copy in gather:
        copy.wait()
    for t, (i, j) in enumerate(upper):
        tile = total[t * WIDE : (t + 1) * WIDE, :]
        out_ref[i * WIDE : (i + 1) * WIDE, j * WIDE : (j + 1) * WIDE] = tile
        if j > i:
            out_ref[j * WIDE : (j + 1) * WIDE, i * WIDE : (i + 1) * WIDE] = tile.T


def summed(gram, peers):
    n = gram.shape[0]
    tiles = n // WIDE
    deep = tiles * (tiles + 1) // 2 * WIDE
    return pl.pallas_call(
        functools.partial(sum_kernel, peers),
        out_shape=jax.ShapeDtypeStruct((n, n), jnp.float32),
        in_specs=[pl.BlockSpec(memory_space=pltpu.VMEM)],
        out_specs=pl.BlockSpec(memory_space=pltpu.VMEM),
        scratch_shapes=[
            pltpu.VMEM((deep, WIDE), jnp.float32),
            pltpu.VMEM((deep, WIDE), jnp.float32),
            pltpu.VMEM((peers - 1, deep // peers, WIDE), jnp.float32),
            pltpu.SemaphoreType.DMA((4, peers - 1)),
        ],
        compiler_params=pltpu.CompilerParams(
            collective_id=0, has_side_effects=True, vmem_limit_bytes=32 * 2**20
        ),
    )(gram)


def pack_kernel(order_ref, src_ref, dst_ref):
    for i in range(order_ref.shape[0]):
        at = pl.ds(pl.multiple_of(order_ref[i] * BLK, BLK), BLK)
        dst_ref[i // 2, :, pl.ds(i % 2 * BLK, BLK)] = src_ref[:, at]


def unpack_kernel(order_ref, src_ref, dst_ref):
    for i in range(order_ref.shape[0]):
        at = pl.ds(pl.multiple_of(order_ref[i] * BLK, BLK), BLK)
        dst_ref[:, at] = src_ref[i // 2, :, pl.ds(i % 2 * BLK, BLK)]


def move_blocks(kernel, array, order, shape):
    return pl.pallas_call(
        kernel,
        out_shape=jax.ShapeDtypeStruct(shape, jnp.float32),
        in_specs=[
            pl.BlockSpec(memory_space=pltpu.SMEM),
            pl.BlockSpec(memory_space=pltpu.VMEM),
        ],
        out_specs=pl.BlockSpec(memory_space=pltpu.VMEM),
        compiler_params=pltpu.CompilerParams(vmem_limit_bytes=48 * 2**20),
    )(order, array)


def pack_blocks(matrix, order):
    rows, width = matrix.shape
    return move_blocks(pack_kernel, matrix, order, (width // (2 * BLK), rows, 2 * BLK))


def unpack_blocks(packed, order):
    pairs, rows, span = packed.shape
    return move_blocks(unpack_kernel, packed, order, (rows, pairs * span))


def in_group(low):
    me = lax.axis_index("rows") * low + lax.axis_index("low")
    return me, lambda at: {"rows": at // low, "low": at % low}


def greet(count, me, where):
    barrier = pltpu.get_barrier_semaphore()

    def signal(k, carry):
        pl.semaphore_signal(
            barrier,
            inc=1,
            device_id=where((me + k) % count),
            device_id_type=pl.DeviceIdType.MESH,
        )
        return carry

    lax.fori_loop(1, count, signal, 0)
    pl.semaphore_wait(barrier, count - 1)


def chunk_copy(src, dst, sems, k, me, count, where):
    at = (me + k) % count
    return pltpu.make_async_remote_copy(
        src_ref=src.at[at],
        dst_ref=dst.at[me],
        send_sem=sems.at[0, k],
        recv_sem=sems.at[1, k],
        device_id=where(at),
        device_id_type=pl.DeviceIdType.MESH,
    )


def spread_kernel(low, packed, out_ref, sems):
    count = out_ref.shape[0]
    me, where = in_group(low)
    greet(count, me, where)

    def start(k, carry):
        chunk_copy(packed, out_ref, sems, k, me, count, where).start()
        return carry

    def wait(k, carry):
        chunk_copy(packed, out_ref, sems, k, me, count, where).wait()
        return carry

    lax.fori_loop(1, count, start, 0)
    out_ref[me] = packed[me]
    lax.fori_loop(1, count, wait, 0)


def spread(packed, low):
    return pl.pallas_call(
        functools.partial(spread_kernel, low),
        out_shape=jax.ShapeDtypeStruct(packed.shape, jnp.float32),
        in_specs=[pl.BlockSpec(memory_space=pltpu.VMEM)],
        out_specs=pl.BlockSpec(memory_space=pltpu.VMEM),
        scratch_shapes=[pltpu.SemaphoreType.DMA((2, packed.shape[0]))],
        compiler_params=pltpu.CompilerParams(
            collective_id=1, has_side_effects=True, vmem_limit_bytes=48 * 2**20
        ),
    )(packed)


def return_kernel(low, cols_ref, turn_ref, landed, turned, sems):
    count = cols_ref.shape[0]
    me, where = in_group(low)
    greet(count, me, where)

    def start(k, carry):
        at = (me + k) % count
        turned[at] = mul(cols_ref[at], turn_ref[...], ((1,), (1,)))
        chunk_copy(turned, landed, sems, k, me, count, where).start()
        return carry

    def wait(k, carry):
        chunk_copy(turned, landed, sems, k, me, count, where).wait()
        return carry

    lax.fori_loop(1, count, start, 0)
    landed[me] = mul(cols_ref[me], turn_ref[...], ((1,), (1,)))
    lax.fori_loop(1, count, wait, 0)


def turn_back(owned, turn, low):
    return pl.pallas_call(
        functools.partial(return_kernel, low),
        out_shape=jax.ShapeDtypeStruct(owned.shape, jnp.float32),
        in_specs=[
            pl.BlockSpec(memory_space=pltpu.VMEM),
            pl.BlockSpec(memory_space=pltpu.VMEM),
        ],
        out_specs=pl.BlockSpec(memory_space=pltpu.VMEM),
        scratch_shapes=[
            pltpu.VMEM(owned.shape, jnp.float32),
            pltpu.SemaphoreType.DMA((2, owned.shape[0])),
        ],
        compiler_params=pltpu.CompilerParams(
            collective_id=2, has_side_effects=True, vmem_limit_bytes=48 * 2**20
        ),
    )(owned, turn)


def pair_places(rows, low):
    path = [0, 1, 3, 2] if rows == 4 else list(range(rows))
    places = []
    for at in range(low):
        places += [r * low + at for r in (path if at % 2 == 0 else path[::-1])]
    return places


GROUP = ("rows", "low")


def turn_of(owned_pair, high):
    return rotation_of(summed(gram_of(owned_pair), high))


def make_body(rows, high, low):
    count = rows * low
    places = pair_places(rows, low)
    pair_at = np.argsort(np.array(places))
    slots = np.stack([2 * pair_at, 2 * pair_at + 1], axis=1).reshape(-1)
    ring = [(places[k], places[(k + 1) % count]) for k in range(count)]

    def body(upper, matching):
        deep = upper.shape[0]
        chunks = spread(pack_blocks(upper, matching[0][slots]), low)
        owned = chunks.reshape(count * deep, 2 * BLK)
        owned = mul(owned, turn_of(owned, high), ((1,), (1,)))
        second = lax.ppermute(owned[:, BLK:], GROUP, ring)
        owned = jnp.concatenate([owned[:, :BLK], second], axis=1)
        turn = turn_of(owned, high)
        returned = turn_back(owned.reshape(count, deep, 2 * BLK), turn, low)
        return unpack_blocks(returned, matching[1][slots])

    return body


def solution(mesh):
    rows, cols = mesh.shape["rows"], mesh.shape["cols"]
    low = cols // rows
    high = cols // low
    split = jax.sharding.Mesh(mesh.devices.reshape(rows, high, low), ("rows", "high", "low"))
    spec = P(("rows", "high", "low"), None)
    return jax.shard_map(
        make_body(rows, high, low), mesh=split, in_specs=(spec, P()), out_specs=spec, check_vma=False
    )
```
